256 devices in a mesh: tm: 8 (over z_lo, x), height: 32 (over z_hi, y, core).
Axes of the slice: x: 4, y: 4, z: 8 (z_hi: 4, z_lo: 2; z = z_hi * 2 + z_lo), core: 2. Of those that a mesh axis runs over, the one named last changes fastest.
Arguments:
- inputs: bfloat16 [16, 768, 4, 1024], P('tm', 'height'), may hold values from -24 to 24
- w_query: bfloat16 [1024, 1024], replicated, may hold values from -0.1875 to 0.1875
- w_key: bfloat16 [1024, 1024], replicated, may hold values from -0.1875 to 0.1875
- w_value: bfloat16 [1024, 1024], replicated, may hold values from -0.1875 to 0.1875
- w_out: bfloat16 [1024, 1024], replicated, may hold values from -0.1875 to 0.1875
- grad_out: bfloat16 [16, 768, 4, 1024], P('tm', 'height'), may hold values from -6 to 6
Outputs:
- attended: bfloat16 [16, 768, 4, 1024], P('tm', 'height')
- grad_in: bfloat16 [16, 768, 4, 1024], P('tm', 'height')
The draws below stay inside these ranges and needn't reach their ends.
All inputs are finite; a program needn't handle non-finite values.
Results may differ from the reference program's by a relative error of at most 0.03.
The reference program's roundings to bfloat16 on the way count: a program that leaves them out, or rounds other values in their place, can miss the bound.
Values may be sent and summed in bfloat16 or wider, within the bound.
No kernel may reach another device: no remote copies, remote signals or barrier semaphores. Data moves between devices by JAX's collectives and lax.ppermute only.
A program may use at most 128 MiB of HBM per device.

```python
import jax
import jax.numpy as jnp
from jax import lax

D = 1024
HD = 64
RT = 2
RH = 7
RW = 7
HB = 24
WC = 4
NT = 16
NH = 768


def draw_inputs(key, part):
    key = jax.random.fold_in(key, 11)
    shape = (NT, NH, WC, D)
    values = jnp.clip(jax.random.normal(key, shape, jnp.float32), -6.0, 6.0)
    return values.astype(jnp.bfloat16)


def levels(key, shape, cuts, least, largest):
    level, own = 1.0, jax.random.fold_in(key, 6)
    for position, parts in cuts:
        draws = jnp.exp(jax.random.uniform(jax.random.fold_in(own, position), (parts,), jnp.float32, least / len(cuts), largest / len(cuts)))
        level = level * jnp.repeat(draws, shape[position] // parts).reshape([-1 if axis == position else 1 for axis in range(len(shape))])
    return level


def noise(rng, dims, scale, limit, pieces=(), kind=jnp.bfloat16):
    entries = jax.random.normal(rng, dims, jnp.float32) * scale
    if len(pieces) > 0:
        entries = levels(rng, dims, pieces, -0.22, 0.18) * entries
    return jnp.clip(entries, min=-limit, max=limit).astype(kind)


def setup_inputs(seed: int = 0) -> dict:
    arg_keys = jax.random.split(jax.random.key(seed), 7)
    inputs = draw_inputs(jax.random.fold_in(arg_keys[6], 71), 0)
    w_query = noise(arg_keys[1], (D, D), D ** -0.5, 0.1875)
    w_key = noise(arg_keys[2], (D, D), D ** -0.5, 0.1875)
    w_value = noise(arg_keys[3], (D, D), D ** -0.5, 0.1875)
    w_out = noise(arg_keys[4], (D, D), D ** -0.5, 0.1875)
    grad_out = noise(arg_keys[5], (NT, NH, WC, D), 1.0, 6.0, ((0, 8), (1, 32)))
    return {"inputs": inputs, "w_query": w_query, "w_key": w_key, "w_value": w_value, "w_out": w_out, "grad_out": grad_out}


def attend(queries, keyvals, grads, allowed):
    qcount = queries.shape[0]
    kcount = keyvals.shape[0]
    width = queries.shape[1]
    heads = width // HD
    scale = HD ** -0.5
    qh = queries.reshape(qcount, heads, HD).astype(jnp.float32)
    kh = keyvals[:, :width].reshape(kcount, heads, HD).astype(jnp.float32)
    vh = keyvals[:, width:].reshape(kcount, heads, HD).astype(jnp.float32)
    scores = jnp.einsum("qhd,khd->hqk", qh, kh) * scale
    scores = jnp.where(allowed[None], scores, jnp.float32(-1e30))
    top = jnp.max(scores, axis=2, keepdims=True)
    expo = jnp.exp(scores - top)
    probs = expo / jnp.sum(expo, axis=2, keepdims=True)
    probs_b = probs.astype(jnp.bfloat16)
    mixed = jnp.einsum("hqk,khd->qhd", probs_b.astype(jnp.float32), vh).astype(jnp.bfloat16)
    gh = grads.reshape(qcount, heads, HD).astype(jnp.float32)
    delta = jnp.sum(gh * mixed.astype(jnp.float32), axis=2).T
    dprob = jnp.einsum("qhd,khd->hqk", gh, vh)
    dscore = (probs * (dprob - delta[:, :, None]) * scale).astype(jnp.bfloat16).astype(jnp.float32)
    grad_q = jnp.einsum("hqk,khd->qhd", dscore, kh).astype(jnp.bfloat16)
    grad_k = jnp.einsum("hqk,qhd->khd", dscore, qh)
    grad_v = jnp.einsum("hqk,qhd->khd", probs_b.astype(jnp.float32), gh)
    both = jnp.concatenate([grad_k.reshape(kcount, width), grad_v.reshape(kcount, width)], axis=1)
    return mixed.reshape(qcount, width), grad_q.reshape(qcount, width), both


def reference(inputs, w_query, w_key, w_value, w_out, grad_out):
    tokens = inputs.reshape(-1, D)
    query = jnp.dot(tokens, w_query, preferred_element_type=jnp.float32).astype(jnp.bfloat16).reshape(NT, NH, WC, D)
    key = jnp.dot(tokens, w_key, preferred_element_type=jnp.float32).astype(jnp.bfloat16).reshape(NT, NH, WC, D)
    value = jnp.dot(tokens, w_value, preferred_element_type=jnp.float32).astype(jnp.bfloat16).reshape(NT, NH, WC, D)
    grad_att = jnp.dot(grad_out.reshape(-1, D), w_out.T, preferred_element_type=jnp.float32).astype(jnp.bfloat16).reshape(NT, NH, WC, D)
    keyval = jnp.concatenate([key, value], axis=3)
    keyval = jnp.pad(keyval, ((RT, RT), (RH, RH), (0, 0), (0, 0)))
    frame_ok = jnp.pad(jnp.ones((NT,), jnp.int32), (RT, RT))
    row_ok = jnp.pad(jnp.ones((NH,), jnp.int32), (RH, RH))
    qrow = jnp.repeat(jnp.arange(HB), WC)
    qcol = jnp.tile(jnp.arange(WC), HB)
    krow = jnp.repeat(jnp.arange(HB + 2 * RH), WC)
    kcol = jnp.tile(jnp.arange(WC), HB + 2 * RH)
    rdiff = krow[None, :] - qrow[:, None]
    base = (rdiff >= 0) & (rdiff <= 2 * RH) & (jnp.abs(kcol[None, :] - qcol[:, None]) <= RW)
    bands = NH // HB
    span_f = 2 * RT + 1
    span_r = HB + 2 * RH

    def step(carry, index):
        frame = index // bands
        row0 = (index % bands) * HB
        zero = jnp.int32(0)
        qb = lax.dynamic_slice(query, (frame, row0, zero, zero), (1, HB, WC, D)).reshape(HB * WC, D)
        gb = lax.dynamic_slice(grad_att, (frame, row0, zero, zero), (1, HB, WC, D)).reshape(HB * WC, D)
        kvb = lax.dynamic_slice(keyval, (frame, row0, zero, zero), (span_f, span_r, WC, 2 * D))
        fok = lax.dynamic_slice(frame_ok, (frame,), (span_f,)) > 0
        rok = lax.dynamic_slice(row_ok, (row0,), (span_r,)) > 0
        kok = jnp.repeat(rok, WC)
        allowed = base[:, None, :] & kok[None, None, :] & fok[None, :, None]
        allowed = allowed.reshape(HB * WC, span_f * span_r * WC)
        mixed, grad_q, both = attend(qb, kvb.reshape(-1, 2 * D), gb, allowed)
        old = lax.dynamic_slice(carry, (frame, row0, zero, zero), (span_f, span_r, WC, 2 * D))
        carry = lax.dynamic_update_slice(carry, old + both.reshape(span_f, span_r, WC, 2 * D), (frame, row0, zero, zero))
        return carry, (mixed, grad_q)

    start = jnp.zeros((NT + 2 * RT, NH + 2 * RH, WC, 2 * D), jnp.float32)
    total, (mixed_all, gradq_all) = lax.scan(step, start, jnp.arange(NT * bands, dtype=jnp.int32))
    mixed_all = mixed_all.reshape(NT, NH, WC, D)
    gradq_all = gradq_all.reshape(NT, NH, WC, D)
    attended = jnp.dot(mixed_all.reshape(-1, D), w_out, preferred_element_type=jnp.float32).astype(jnp.bfloat16).reshape(NT, NH, WC, D)
    core = total[RT:RT + NT, RH:RH + NH]
    grad_key = core[..., :D].astype(jnp.bfloat16).reshape(-1, D)
    grad_value = core[..., D:].astype(jnp.bfloat16).reshape(-1, D)
    grad_in = jnp.dot(gradq_all.reshape(-1, D), w_query.T, preferred_element_type=jnp.float32)
    grad_in = grad_in + jnp.dot(grad_key, w_key.T, preferred_element_type=jnp.float32)
    grad_in = grad_in + jnp.dot(grad_value, w_value.T, preferred_element_type=jnp.float32)
    return attended, grad_in.astype(jnp.bfloat16).reshape(NT, NH, WC, D)
```

```python
import functools

import jax
import jax.numpy as jnp
from jax import lax
from jax.experimental import pallas as pl
from jax.experimental.pallas import tpu as pltpu
from jax.sharding import PartitionSpec as P

HD = 64
RT = 2
RH = 7
BR = 8
WC = 4
GW = 256
VMEM_LIMIT = 56 * 1024 * 1024
NEG = -1e30
F32 = jnp.float32
BF16 = jnp.bfloat16


def nn(a, b):
    return lax.dot_general(a, b, (((1,), (0,)), ((), ())), preferred_element_type=F32)


def nt(a, b):
    return lax.dot_general(a, b, (((1,), (1,)), ((), ())), preferred_element_type=F32)


def tn(a, b):
    return lax.dot_general(a, b, (((0,), (0,)), ((), ())), preferred_element_type=F32)


def call(body, out_shapes, *args, scalars=False, scratch=()):
    specs = [pl.BlockSpec(memory_space=pltpu.VMEM) for _ in args]
    if scalars:
        specs[0] = pl.BlockSpec(memory_space=pltpu.SMEM)
    return pl.pallas_call(
        body,
        out_shape=[jax.ShapeDtypeStruct(s, d) for s, d in out_shapes],
        in_specs=specs,
        out_specs=[pl.BlockSpec(memory_space=pltpu.VMEM) for _ in out_shapes],
        scratch_shapes=list(scratch),
        compiler_params=pltpu.CompilerParams(vmem_limit_bytes=VMEM_LIMIT),
    )(*args)


def project(x, w_ref, out_ref, scale=None):
    groups, frames, rows, width = out_ref.shape
    for g in range(groups):
        y = nn(x, w_ref[:, g * width : (g + 1) * width])
        if scale is not None:
            y = y * scale
        out_ref[g] = y.astype(BF16).reshape(frames, rows, width)


def project_t(x, w_ref, out_ref):
    groups, frames, rows, width = out_ref.shape
    for g in range(groups):
        y = nt(x, w_ref[g * width : (g + 1) * width, :])
        out_ref[g] = y.astype(BF16).reshape(frames, rows, width)


def flat(ref):
    return ref[...].reshape(-1, ref.shape[-1])


def own_kernel(x_ref, gr_ref, wq_ref, wk_ref, wv_ref, wo_ref, q_ref, k_ref, v_ref, ga_ref):
    x = flat(x_ref)
    project(x, wk_ref, k_ref)
    project(x, wv_ref, v_ref)
    project(x, wq_ref, q_ref, HD**-0.5)
    project_t(flat(gr_ref), wo_ref, ga_ref)


def side_kernel(xa_ref, xb_ref, wq_ref, wk_ref, wv_ref, q_ref, k_ref, v_ref):
    x = jnp.concatenate([flat(xa_ref), flat(xb_ref)], axis=0)
    project(x, wk_ref, k_ref)
    project(x, wv_ref, v_ref)
    project(x, wq_ref, q_ref, HD**-0.5)


def side_grad_kernel(ga_ref, gb_ref, wo_ref, out_ref):
    g = jnp.concatenate([flat(ga_ref), flat(gb_ref)], axis=0)
    project_t(g, wo_ref, out_ref)


def spread(block):
    heads = block.shape[1] // HD
    lane = lax.broadcasted_iota(jnp.int32, block.shape, 1) // HD
    zero = jnp.zeros_like(block)
    return jnp.concatenate([jnp.where(lane == h, block, zero) for h in range(heads)], axis=0)


def window(rb, own, top, bottom):
    half = BR * WC
    if rb == 0:
        return jnp.concatenate([top, own[:, : 2 * half]], axis=1)
    if rb == 1:
        return own
    return jnp.concatenate([own[:, half:], bottom], axis=1)


def row_bias(rb, h, n_rows, rows):
    span = 3 * BR * WC
    w = lax.broadcasted_iota(jnp.int32, (span, GW), 0) // WC
    r = (lax.broadcasted_iota(jnp.int32, (span, GW), 1) % (BR * WC)) // WC
    diff = w - r - BR
    glob = h * rows + rb * BR + w - BR
    ok = (diff >= -RH) & (diff <= RH) & (glob >= 0) & (glob < n_rows)
    return jnp.where(ok, F32(0), F32(NEG))


def frame_bias(key_off, query_off, tm, n_frames, frames):
    fq = (lax.broadcasted_iota(jnp.int32, (1, GW), 1) // (BR * WC)) % 2 + query_off
    diff = key_off - fq
    glob = tm * frames + key_off
    ok = (diff >= -RT) & (diff <= RT) & (glob >= 0) & (glob < n_frames)
    return jnp.where(ok, F32(0), F32(NEG))


def slot_offsets(tm):
    odd = tm % 2
    return 4 * odd - 2, 2 - 4 * odd


def forward_kernel(
    n_frames, n_rows, frames, rows,
    info_ref, xe_ref, xo_ref, wk_ref, wv_ref, q_ref, ga_ref, k_ref, v_ref, ks_ref, vs_ref,
    stats_ref, mixed_ref, dq_ref, dk_ref, dv_ref, krow_ref, vrow_ref,
    bias_ref, kh_ref, vh_ref,
):
    tm, h = info_ref[0], info_ref[1]
    half = BR * WC
    groups = q_ref.shape[0]
    h_odd = h % 2
    for x_ref, side in ((xe_ref, 1 - h_odd), (xo_ref, h_odd)):
        x = flat(x_ref)
        for g in range(groups):
            kh_ref[side, g] = nn(x, wk_ref[:, g * GW : (g + 1) * GW]).astype(BF16).reshape(6, half, GW)
            vh_ref[side, g] = nn(x, wv_ref[:, g * GW : (g + 1) * GW]).astype(BF16).reshape(6, half, GW)
    for side in range(2):
        for g in range(groups):
            krow_ref[side, g] = kh_ref[side, g, 2:4]
            vrow_ref[side, g] = vh_ref[side, g, 2:4]
    off_a, off_b = slot_offsets(tm)
    offsets = (off_a, off_a + 1, 0, 1, off_b, off_b + 1)
    for rb in range(3):
        base = row_bias(rb, h, n_rows, rows)
        for s in range(6):
            bias_ref[rb, s] = base + frame_bias(offsets[s], 0, tm, n_frames, frames)
    dk_ref[...] = jnp.zeros_like(dk_ref)
    dv_ref[...] = jnp.zeros_like(dv_ref)
    pick = (
        lax.broadcasted_iota(jnp.int32, (64, GW), 0) == lax.broadcasted_iota(jnp.int32, (64, GW), 1) % 64
    ).astype(F32).astype(BF16)
    diag = (
        lax.broadcasted_iota(jnp.int32, (GW, GW), 0) // HD == lax.broadcasted_iota(jnp.int32, (GW, GW), 1) // 64
    )

    def group(g, carry):
        kall = jnp.concatenate([ks_ref[g, 0:2], k_ref[g], ks_ref[g, 2:4]], axis=0)
        vall = jnp.concatenate([vs_ref[g, 0:2], v_ref[g], vs_ref[g, 2:4]], axis=0)
        for rb in range(3):
            at = slice(rb * half, (rb + 1) * half)
            kw = window(rb, kall, kh_ref[0, g], kh_ref[1, g]).reshape(-1, GW)
            vw = window(rb, vall, vh_ref[0, g], vh_ref[1, g]).reshape(-1, GW)
            qs = spread(q_ref[g, :, at, :].reshape(64, GW))
            gs = spread(ga_ref[g, :, at, :].reshape(64, GW))
            s = nt(kw, qs) + bias_ref[rb].reshape(-1, GW)
            m = jnp.max(s, axis=0, keepdims=True)
            e = jnp.exp(s - m)
            rl = 1.0 / jnp.sum(e, axis=0, keepdims=True)
            dp = nt(vw, gs)
            delta = jnp.sum(e * dp, axis=0, keepdims=True) * rl
            p = e * rl
            pb = p.astype(BF16)
            ds = (p * (dp - delta)).astype(BF16)
            u = g * 3 + rb
            stats_ref[u, 0:1, :] = m
            stats_ref[u, 1:2, :] = rl
            stats_ref[u, 2:3, :] = delta
            stats_ref[u, 3:4, :] = delta
            mt = jnp.where(diag, tn(vw, pb), 0.0).astype(BF16)
            mixed_ref[g, :, at, :] = nt(pick, mt).astype(BF16).reshape(2, half, GW)
            qt = jnp.where(diag, tn(kw, ds) * (HD**-0.5), 0.0).astype(BF16)
            dq_ref[g, :, at, :] = nt(pick, qt).astype(BF16).reshape(2, half, GW)
            mid = slice(2 * 3 * half, 4 * 3 * half)
            to = slice(rb * half, (rb + 3) * half)
            dk_ref[g, :, to, :] += nn(ds[mid], qs).reshape(2, 3 * half, GW)
            dv_ref[g, :, to, :] += nn(pb[mid], gs).reshape(2, 3 * half, GW)
        return carry

    lax.fori_loop(0, groups, group, 0)


def middle_kernel(mixed_ref, dq_ref, wo_ref, wq_ref, att_ref, dxq_ref):
    groups = mixed_ref.shape[0]
    mixed = jnp.concatenate([mixed_ref[g].reshape(-1, GW) for g in range(groups)], axis=1)
    att_ref[...] = nn(mixed, wo_ref[...]).astype(BF16).reshape(att_ref.shape)
    dq = jnp.concatenate([dq_ref[g].reshape(-1, GW) for g in range(groups)], axis=1)
    dxq_ref[...] = nt(dq, wq_ref[...]).reshape(dxq_ref.shape)


def backward_kernel(
    n_frames, n_rows, frames, rows,
    info_ref, sa_ref, sb_ref, qs_ref, gs_ref, k_ref, v_ref, krow_ref, vrow_ref, dk_ref, dv_ref, dxq_ref,
    wk_ref, wv_ref,
    own_ref, me_ref, mo_ref,
    bias_ref, dka_ref, dva_ref, edge_ref,
):
    tm, h = info_ref[0], info_ref[1]
    half = BR * WC
    groups = k_ref.shape[0]
    off_a, off_b = slot_offsets(tm)
    for rb in range(3):
        base = row_bias(rb, h, n_rows, rows)
        for p, off in enumerate((off_a, off_b)):
            for f in range(2):
                bias_ref[p, rb, f] = base + frame_bias(f, off, tm, n_frames, frames)
    dka_ref[...] = dk_ref[...]
    dva_ref[...] = dv_ref[...]

    def group(g, carry):
        for rb in range(3):
            at = slice(rb * half, (rb + 1) * half)
            to = slice(rb * half, (rb + 3) * half)
            kw = window(rb, k_ref[g], krow_ref[0, g], krow_ref[1, g]).reshape(-1, GW)
            vw = window(rb, v_ref[g], vrow_ref[0, g], vrow_ref[1, g]).reshape(-1, GW)
            u = g * 3 + rb
            for p, s_ref in enumerate((sa_ref, sb_ref)):
                qs = spread(qs_ref[g, 2 * p : 2 * p + 2, at, :].reshape(64, GW))
                gs = spread(gs_ref[g, 2 * p : 2 * p + 2, at, :].reshape(64, GW))
                m, rl, delta = s_ref[u, 0:1, :], s_ref[u, 1:2, :], s_ref[u, 2:3, :]
                s = nt(kw, qs) + bias_ref[p, rb].reshape(-1, GW)
                pr = jnp.exp(s - m) * rl
                ds = (pr * (nt(vw, gs) - delta)).astype(BF16)
                dka_ref[g, :, to, :] += nn(ds, qs).reshape(2, 3 * half, GW)
                dva_ref[g, :, to, :] += nn(pr.astype(BF16), gs).reshape(2, 3 * half, GW)
        return carry

    lax.fori_loop(0, groups, group, 0)
    dk = jnp.concatenate([dka_ref[g].astype(BF16).reshape(-1, GW) for g in range(groups)], axis=1)
    dv = jnp.concatenate([dva_ref[g].astype(BF16).reshape(-1, GW) for g in range(groups)], axis=1)
    dx = (nt(dk, wk_ref[...]) + nt(dv, wv_ref[...])).reshape(2, 5 * half, -1)
    own_ref[...] = dx[:, half : 4 * half] + dxq_ref[...]
    edge_ref[0] = dx[:, :half].astype(BF16)
    edge_ref[1] = dx[:, 4 * half :].astype(BF16)
    h_odd = h % 2
    me_ref[...] = edge_ref[1 - h_odd]
    mo_ref[...] = edge_ref[h_odd]


def last_kernel(info_ref, own_ref, re_ref, ro_ref, out_ref, acc_ref):
    half = BR * WC
    h_odd = info_ref[1] % 2
    acc_ref[...] = own_ref[...]
    for r_ref, side in ((re_ref, 1 - h_odd), (ro_ref, h_odd)):
        at = pl.ds(pl.multiple_of(side * (2 * half), half), half)
        acc_ref[:, at, :] += r_ref[...].astype(F32)
    out_ref[...] = acc_ref[...].astype(BF16)


def swap_pairs(count, first):
    pairs = [(i, i + 1) for i in range(first, count - 1, 2)]
    return pairs + [(b, a) for a, b in pairs]


def swap(block, axis, first):
    return lax.ppermute(block, axis, swap_pairs(lax.axis_size(axis), first))


def shards(inputs, w_query, w_key, w_value, w_out, grad_out):
    frames, rows, cols, width = inputs.shape
    groups = width // GW
    tokens = rows * cols
    half = BR * WC
    tm, h = lax.axis_index("tm"), lax.axis_index("height")
    n_frames, n_rows = lax.axis_size("tm") * frames, lax.axis_size("height") * rows
    info = jnp.stack([tm, h]).astype(jnp.int32)
    dims = (n_frames, n_rows, frames, rows)

    x = inputs.reshape(frames, tokens, width)
    grad = grad_out.reshape(frames, tokens, width)
    xa = swap(x, "tm", 1)
    xb = swap(x, "tm", 0)
    ga = swap(grad, "tm", 1)
    gb = swap(grad, "tm", 0)

    def edge(block, bottom):
        return lax.dynamic_slice_in_dim(block, bottom * (tokens - half), half, axis=1)

    h_odd = h % 2
    wide = jnp.concatenate([xa, x, xb], axis=0)
    xo = swap(edge(wide, h_odd), "height", 1)
    xe = swap(edge(wide, 1 - h_odd), "height", 0)

    group_shape = ((groups, frames, tokens, GW), BF16)
    side_shape = ((groups, 2 * frames, tokens, GW), BF16)
    q, k, v, ga_own = call(own_kernel, [group_shape] * 4, x, grad, w_query, w_key, w_value, w_out)
    q_side, k_side, v_side = call(side_kernel, [side_shape] * 3, xa, xb, w_query, w_key, w_value)
    (ga_side,) = call(side_grad_kernel, [side_shape], ga, gb, w_out)

    acc_shape = (groups, frames, tokens + 2 * half, GW)
    row_shape = ((2, groups, frames, half, GW), BF16)
    stats, mixed, dq, dk, dv, k_row, v_row = call(
        functools.partial(forward_kernel, *dims),
        [((3 * groups, 4, GW), F32), group_shape, group_shape, (acc_shape, F32), (acc_shape, F32), row_shape, row_shape],
        info, xe, xo, w_key, w_value, q, ga_own, k, v, k_side, v_side,
        scalars=True,
        scratch=[
            pltpu.VMEM((3, 6, tokens, GW), F32),
            pltpu.VMEM((2, groups, 6, half, GW), BF16),
            pltpu.VMEM((2, groups, 6, half, GW), BF16),
        ],
    )
    sa = swap(stats, "tm", 1)
    sb = swap(stats, "tm", 0)
    token_shape = (frames, tokens, width)
    attended, dxq = call(
        middle_kernel, [(token_shape, BF16), (token_shape, F32)], mixed, dq, w_out, w_query
    )
    own, me, mo = call(
        functools.partial(backward_kernel, *dims),
        [(token_shape, F32), ((frames, half, width), BF16), ((frames, half, width), BF16)],
        info, sa, sb, q_side, ga_side, k, v, k_row, v_row, dk, dv, dxq, w_key, w_value,
        scalars=True,
        scratch=[
            pltpu.VMEM((2, 3, 2, tokens, GW), F32),
            pltpu.VMEM(acc_shape, F32),
            pltpu.VMEM(acc_shape, F32),
            pltpu.VMEM((2, frames, half, width), BF16),
        ],
    )
    ro = swap(mo, "height", 1)
    re = swap(me, "height", 0)
    (grad_in,) = call(
        last_kernel, [(token_shape, BF16)], info, own, re, ro, scalars=True, scratch=[pltpu.VMEM(token_shape, F32)]
    )
    return (attended.reshape(inputs.shape), grad_in.reshape(inputs.shape))


def solution(mesh):
    placed = (P("tm", "height", None, None), P(), P(), P(), P(), P("tm", "height", None, None))
    return jax.shard_map(
        shards,
        mesh=mesh,
        in_specs=placed,
        out_specs=(P("tm", "height", None, None), P("tm", "height", None, None)),
        check_vma=False,
    )
```

```python
import functools

import jax
import jax.numpy as jnp
from jax import lax
from jax.experimental import pallas as pl
from jax.experimental.pallas import tpu as pltpu
from jax.sharding import PartitionSpec as P

HD = 64
RT = 2
RH = 7
BR = 8
WC = 4
GW = 256
HALF = BR * WC
PER = 4
VMEM_LIMIT = 28 * 1024 * 1024
NEG = -1e30
F32 = jnp.float32
BF16 = jnp.bfloat16


def nn(a, b):
    return lax.dot_general(a, b, (((1,), (0,)), ((), ())), preferred_element_type=F32)


def nt(a, b):
    return lax.dot_general(a, b, (((1,), (1,)), ((), ())), preferred_element_type=F32)


def tn(a, b):
    return lax.dot_general(a, b, (((0,), (0,)), ((), ())), preferred_element_type=F32)


def call(body, out_shapes, *args, places=None, scratch=(), limit=VMEM_LIMIT):
    places = places or {}
    return pl.pallas_call(
        body,
        out_shape=[jax.ShapeDtypeStruct(s, d) for s, d in out_shapes],
        in_specs=[pl.BlockSpec(memory_space=places.get(i, pltpu.VMEM)) for i in range(len(args))],
        out_specs=[pl.BlockSpec(memory_space=pltpu.VMEM) for _ in out_shapes],
        scratch_shapes=list(scratch),
        compiler_params=pltpu.CompilerParams(vmem_limit_bytes=limit),
    )(*args)


def store_blocks(y, out_ref, g):
    frames, blocks, half, _ = y.shape
    for b in range(blocks):
        for f in range(frames):
            at = slice((f % 2) * half, (f % 2 + 1) * half)
            if len(out_ref.shape) == 4:
                out_ref[g, b, at, :] = y[f, b]
            else:
                out_ref[g, f // 2, b, at, :] = y[f, b]


def project(x, w_ref, out_ref, scale=None):
    for g in range(out_ref.shape[0]):
        y = nn(x, w_ref[:, g * GW : (g + 1) * GW])
        if scale is not None:
            y = y * scale
        store_blocks(y.astype(BF16).reshape(-1, 3, HALF, GW), out_ref, g)


def project_t(x, w_ref, out_ref):
    for g in range(out_ref.shape[0]):
        y = nt(x, w_ref[g * GW : (g + 1) * GW, :])
        store_blocks(y.astype(BF16).reshape(-1, 3, HALF, GW), out_ref, g)


def flat(ref):
    return ref[...].reshape(-1, ref.shape[-1])


def own_kernel(
    n_frames, n_rows, frames, rows,
    info_ref, x_ref, gr_ref, wq_hbm, wk_hbm, wv_hbm, wo_hbm,
    q_ref, k_ref, v_ref, ga_ref, wq_ref, wk_ref, wv_ref, wo_ref, fb_ref, bb_ref,
    sem,
):
    pairs = ((wk_hbm, wk_ref), (wv_hbm, wv_ref), (wq_hbm, wq_ref), (wo_hbm, wo_ref))
    copies = [pltpu.make_async_copy(src, dst, sem.at[i]) for i, (src, dst) in enumerate(pairs)]
    for c in copies:
        c.start()
    tm, h = info_ref[0], info_ref[1]
    off_a, off_b = slot_offsets(tm)
    offsets = (off_a, off_a + 1, 0, 1, off_b, off_b + 1)
    for rb in range(3):
        for j in range(3):
            base = row_bias(rb, j, h, n_rows, rows)
            for s in range(6):
                at = (j * 6 + s) * HALF
                fb_ref[rb, at : at + HALF] = base + frame_bias(offsets[s], 0, tm, n_frames, frames)
            for p, off in enumerate((off_a, off_b)):
                for f in range(2):
                    at = (j * 2 + f) * HALF
                    bb_ref[p, rb, at : at + HALF] = base + frame_bias(f, off, tm, n_frames, frames)
    x = flat(x_ref)
    copies[0].wait()
    project(x, wk_ref, k_ref)
    copies[1].wait()
    project(x, wv_ref, v_ref)
    copies[2].wait()
    project(x, wq_ref, q_ref, HD**-0.5)
    copies[3].wait()
    project_t(flat(gr_ref), wo_ref, ga_ref)


def edge_kernel(for_odd, info_ref, x_ref, xa_ref, xb_ref, after_ref, out_ref):
    for parity in range(2):

        @pl.when(info_ref[1] % 2 == parity)
        def _(start=2 * HALF * (parity if for_odd else 1 - parity)):
            for s, ref in enumerate((xa_ref, x_ref, xb_ref)):
                out_ref[2 * s : 2 * s + 2] = ref[:, start : start + HALF]


def side_kernel(xa_ref, xb_ref, wq_ref, wk_ref, wv_ref, after_ref, q_ref, k_ref, v_ref):
    x = jnp.concatenate([flat(xa_ref), flat(xb_ref)], axis=0)
    project(x, wk_ref, k_ref)
    project(x, wv_ref, v_ref)
    project(x, wq_ref, q_ref, HD**-0.5)


def side_grad_kernel(ga_ref, gb_ref, wo_ref, after_ref, out_ref):
    project_t(jnp.concatenate([flat(ga_ref), flat(gb_ref)], axis=0), wo_ref, out_ref)


def spread(block):
    heads = block.shape[1] // HD
    lane = lax.broadcasted_iota(jnp.int32, block.shape, 1) // HD
    zero = jnp.zeros_like(block)
    return jnp.concatenate([jnp.where(lane == h, block, zero) for h in range(heads)], axis=0)


def row_bias(rb, j, h, n_rows, rows):
    w = j * BR + lax.broadcasted_iota(jnp.int32, (HALF, GW), 0) // WC
    r = (lax.broadcasted_iota(jnp.int32, (HALF, GW), 1) % HALF) // WC
    diff = w - r - BR
    glob = h * rows + rb * BR + w - BR
    ok = (diff >= -RH) & (diff <= RH) & (glob >= 0) & (glob < n_rows)
    return jnp.where(ok, F32(0), F32(NEG))


def frame_bias(key_off, query_off, tm, n_frames, frames):
    fq = (lax.broadcasted_iota(jnp.int32, (1, GW), 1) // HALF) % 2 + query_off
    diff = key_off - fq
    glob = tm * frames + key_off
    ok = (diff >= -RT) & (diff <= RT) & (glob >= 0) & (glob < n_frames)
    return jnp.where(ok, F32(0), F32(NEG))


def slot_offsets(tm):
    odd = tm % 2
    return 4 * odd - 2, 2 - 4 * odd


def pipeline(count, *stages):
    held = {}
    for t in range(count + len(stages) - 1):
        for s, stage in enumerate(stages):
            u = t - s
            if 0 <= u < count:
                held[u] = stage(u, held.get(u))


def forward_kernel(
    info_ref, xe_ref, xo_ref, wk_ref, wv_ref, q_ref, ga_ref, k_ref, v_ref, ks_ref, vs_ref, bias_ref, after_ref,
    stats_ref, mixed_ref, dq_ref, dk_ref, dv_ref, krow_ref, vrow_ref,
    kh_ref, vh_ref,
):
    groups = q_ref.shape[0]
    own = slice(2 * HALF, 4 * HALF)
    h_odd = info_ref[1] % 2
    for x_ref, side in ((xe_ref, 1 - h_odd), (xo_ref, h_odd)):
        x = flat(x_ref)
        for g in range(groups):
            kh_ref[side, g] = nn(x, wk_ref[:, g * GW : (g + 1) * GW]).astype(BF16)
            vh_ref[side, g] = nn(x, wv_ref[:, g * GW : (g + 1) * GW]).astype(BF16)
    for side in range(2):
        for g in range(groups):
            krow_ref[side, g] = kh_ref[side, g, own]
            vrow_ref[side, g] = vh_ref[side, g, own]
    dk_ref[...] = jnp.zeros_like(dk_ref)
    dv_ref[...] = jnp.zeros_like(dv_ref)
    diag = (
        lax.broadcasted_iota(jnp.int32, (GW, GW), 0) // HD == lax.broadcasted_iota(jnp.int32, (GW, GW), 1) // 64
    )

    def some(i, carry):
        cache = {}

        def blocks(g, which, margin_ref, side_ref, own_ref):
            if (g, which) not in cache:
                at = i * PER + g
                mid = [jnp.concatenate([side_ref[at, 0, b], own_ref[at, b], side_ref[at, 1, b]], axis=0) for b in range(3)]
                cache[g, which] = [margin_ref[0, at], *mid, margin_ref[1, at]]
            return cache[g, which]

        def flipped(g, which, b, block):
            if (g, which, b) not in cache:
                cache[g, which, b] = block.T
            return cache[g, which, b]

        def scores(u, _):
            g, rb = u // 3, u % 3
            kb = blocks(g, 0, kh_ref, ks_ref, k_ref)[rb : rb + 3]
            vb = blocks(g, 1, vh_ref, vs_ref, v_ref)[rb : rb + 3]
            kt = [flipped(g, 0, rb + j, kb[j]) for j in range(3)]
            vt = [flipped(g, 1, rb + j, vb[j]) for j in range(3)]
            qs, gs = spread(q_ref[i * PER + g, rb]), spread(ga_ref[i * PER + g, rb])
            s = nt(jnp.concatenate(kb, axis=0), qs)
            dp = nt(jnp.concatenate(vb, axis=0), gs)
            return kt, vt, qs, gs, s, dp

        def soft(u, held):
            rb = u % 3
            kt, vt, qs, gs, s, dp = held
            s = s + bias_ref[rb]
            m = jnp.max(s, axis=0, keepdims=True)
            e = jnp.exp(s - m)
            rl = 1.0 / jnp.sum(e, axis=0, keepdims=True)
            delta = jnp.sum(e * dp, axis=0, keepdims=True) * rl
            p = e * rl
            row = i * (3 * PER) + u
            stats_ref[row, 0:1, :] = m
            stats_ref[row, 1:2, :] = rl
            stats_ref[row, 2:3, :] = delta
            stats_ref[row, 3:4, :] = delta
            return kt, vt, qs, gs, p.astype(BF16), (p * (dp - delta)).astype(BF16)

        def back(u, held):
            g, rb = i * PER + u // 3, u % 3
            kt, vt, qs, gs, pb, ds = held

            def gather(t, p):
                parts = [nn(t[j], p[j * 6 * HALF : (j + 1) * 6 * HALF]) for j in range(3)]
                return parts[0] + parts[1] + parts[2]

            def fold(y):
                y = jnp.where(diag, y, 0.0)
                y = (y[:, : GW // 2] + y[:, GW // 2 :]).astype(BF16).T
                return y[:64] + y[64:]

            mixed_ref[g, rb] = fold(gather(vt, pb))
            dq_ref[g, rb] = fold(gather(kt, ds) * (HD**-0.5))

            def middle(p):
                return jnp.concatenate([p[(j * 6 + 2) * HALF : (j * 6 + 4) * HALF] for j in range(3)], axis=0)

            dk_ref[g, rb : rb + 3] += nn(middle(ds), qs).reshape(3, 2 * HALF, GW)
            dv_ref[g, rb : rb + 3] += nn(middle(pb), gs).reshape(3, 2 * HALF, GW)

        pipeline(3 * PER, scores, soft, back)
        return carry

    lax.fori_loop(0, groups // PER, some, 0)


def unblock(y, out_ref):
    for b in range(3):
        for f in range(out_ref.shape[0]):
            part = y[b, f * HALF : (f + 1) * HALF].astype(out_ref.dtype)
            if len(out_ref.shape) == 3:
                out_ref[f, b * HALF : (b + 1) * HALF, :] = part
            else:
                out_ref[f, b * BR : (b + 1) * BR] = part.reshape(BR, WC, -1)


def middle_kernel(mixed_ref, dq_ref, wo_ref, wq_ref, att_ref, dxq_ref):
    groups = mixed_ref.shape[0]
    mixed = jnp.concatenate([flat(mixed_ref.at[g]) for g in range(groups)], axis=1)
    unblock(nn(mixed, wo_ref[...]).reshape(3, 2 * HALF, -1), att_ref)
    dq = jnp.concatenate([flat(dq_ref.at[g]) for g in range(groups)], axis=1)
    dxq_ref[...] = nt(dq, wq_ref[...]).reshape(dxq_ref.shape)


def margin_kernel(
    info_ref, sa_ref, sb_ref, qs_ref, gs_ref, krow_ref, vrow_ref, dk_ref, dv_ref, bias_ref, wk_ref, wv_ref, after_ref,
    me_ref, mo_ref,
    dka_ref, dva_ref, edge_ref,
):
    groups = qs_ref.shape[0]
    parts = {}

    def scores(u, _):
        g, side, p = u // 4, u // 2 % 2, u % 2
        qs, gs = spread(qs_ref[g, p, 2 * side]), spread(gs_ref[g, p, 2 * side])
        return qs, gs, nt(krow_ref[side, g], qs), nt(vrow_ref[side, g], gs)

    def soft(u, held):
        g, side, p = u // 4, u // 2 % 2, u % 2
        qs, gs, s, dp = held
        stat_ref, row = (sa_ref, sb_ref)[p], g * 3 + 2 * side
        m, rl, delta = stat_ref[row, 0:1, :], stat_ref[row, 1:2, :], stat_ref[row, 2:3, :]
        at = 4 * side * HALF
        pr = jnp.exp(s + bias_ref[p, 2 * side, at : at + 2 * HALF] - m) * rl
        return qs, gs, (pr * (dp - delta)).astype(BF16), pr.astype(BF16)

    def back(u, held):
        qs, gs, ds, pb = held
        parts[u] = nn(ds, qs), nn(pb, gs)

    pipeline(4 * groups, scores, soft, back)
    for g in range(groups):
        for side in range(2):
            u = 4 * g + 2 * side
            dka_ref[g, side] = (dk_ref[g, 4 * side] + parts[u][0] + parts[u + 1][0]).astype(BF16)
            dva_ref[g, side] = (dv_ref[g, 4 * side] + parts[u][1] + parts[u + 1][1]).astype(BF16)
    dk = jnp.concatenate([flat(dka_ref.at[g]) for g in range(groups)], axis=1)
    dv = jnp.concatenate([flat(dva_ref.at[g]) for g in range(groups)], axis=1)
    dx = (nt(dk, wk_ref[...]) + nt(dv, wv_ref[...])).astype(BF16)
    edge_ref[...] = dx.reshape(edge_ref.shape)
    h_odd = info_ref[1] % 2
    me_ref[...] = edge_ref[1 - h_odd]
    mo_ref[...] = edge_ref[h_odd]


def backward_kernel(
    sa_ref, sb_ref, qs_ref, gs_ref, k_ref, v_ref, dk_ref, dv_ref, dxq_ref, bias_ref, wk_ref, wv_ref,
    own_ref,
    dka_ref, dva_ref,
):
    groups = k_ref.shape[0]
    dka_ref[...] = dk_ref[:, 1:4]
    dva_ref[...] = dv_ref[:, 1:4]
    reach = ((0, 2, 2 * HALF), (0, 3, 0), (1, 3, 0))

    def group(g, carry):
        def scores(u, _):
            rb, p = u // 2, u % 2
            lo, hi, _ = reach[rb]
            qs, gs = spread(qs_ref[g, p, rb]), spread(gs_ref[g, p, rb])
            return qs, gs, nt(flat(k_ref.at[g, lo:hi]), qs), nt(flat(v_ref.at[g, lo:hi]), gs)

        def soft(u, held):
            rb, p = u // 2, u % 2
            qs, gs, s, dp = held
            stat_ref, row, at = (sa_ref, sb_ref)[p], g * 3 + rb, reach[rb][2]
            m, rl, delta = stat_ref[row, 0:1, :], stat_ref[row, 1:2, :], stat_ref[row, 2:3, :]
            pr = jnp.exp(s + bias_ref[p, rb, at : at + s.shape[0]] - m) * rl
            return qs, gs, pr.astype(BF16), (pr * (dp - delta)).astype(BF16)

        def back(u, held):
            lo, hi, _ = reach[u // 2]
            qs, gs, pb, ds = held
            dka_ref[g, lo:hi] += nn(ds, qs).reshape(hi - lo, 2 * HALF, GW)
            dva_ref[g, lo:hi] += nn(pb, gs).reshape(hi - lo, 2 * HALF, GW)

        pipeline(6, scores, soft, back)
        return carry

    lax.fori_loop(0, groups, group, 0)
    dk = jnp.concatenate([flat(dka_ref.at[g]).astype(BF16) for g in range(groups)], axis=1)
    dv = jnp.concatenate([flat(dva_ref.at[g]).astype(BF16) for g in range(groups)], axis=1)
    dx = (nt(dk, wk_ref[...]) + nt(dv, wv_ref[...])).reshape(3, 2 * HALF, -1)
    unblock(dx + dxq_ref[...], own_ref)


def last_kernel(info_ref, own_ref, re_ref, ro_ref, out_ref, acc_ref):
    h_odd = info_ref[1] % 2
    top, bottom = slice(0, HALF), slice(2 * HALF, 3 * HALF)
    acc_ref[...] = own_ref[...]
    for parity, of_even, of_odd in ((0, bottom, top), (1, top, bottom)):

        @pl.when(h_odd == parity)
        def _(of_even=of_even, of_odd=of_odd):
            acc_ref[:, of_even] += re_ref[...].astype(F32)
            acc_ref[:, of_odd] += ro_ref[...].astype(F32)

    out_ref[...] = acc_ref[...].astype(BF16).reshape(out_ref.shape)


def swap_pairs(count, first):
    pairs = [(i, i + 1) for i in range(first, count - 1, 2)]
    return pairs + [(b, a) for a, b in pairs]


def swap(block, axis, first):
    return lax.ppermute(block, axis, swap_pairs(lax.axis_size(axis), first))


def shards(inputs, w_query, w_key, w_value, w_out, grad_out):
    frames, rows, cols, width = inputs.shape
    groups = width // GW
    tokens = rows * cols
    tm, h = lax.axis_index("tm"), lax.axis_index("height")
    n_frames, n_rows = lax.axis_size("tm") * frames, lax.axis_size("height") * rows
    info = jnp.stack([tm, h]).astype(jnp.int32)
    dims = (n_frames, n_rows, frames, rows)

    x = inputs.reshape(frames, tokens, width)
    xa = swap(x, "tm", 1)
    xb = swap(x, "tm", 0)
    grad = grad_out.reshape(frames, tokens, width)
    ga = swap(grad, "tm", 1)
    gb = swap(grad, "tm", 0)

    own_shape = ((groups, 3, 2 * HALF, GW), BF16)
    side_shape = ((groups, 2, 3, 2 * HALF, GW), BF16)
    weight_shape = (w_query.shape, BF16)
    hbm = {i: pltpu.HBM for i in range(3, 7)}
    q, k, v, ga_own, wq, wk, wv, wo, f_bias, b_bias = call(
        functools.partial(own_kernel, *dims),
        [own_shape] * 4 + [weight_shape] * 4 + [((3, 18 * HALF, GW), F32), ((2, 3, 6 * HALF, GW), F32)],
        info, x, grad, w_query, w_key, w_value, w_out,
        places={0: pltpu.SMEM, **hbm},
        scratch=[pltpu.SemaphoreType.DMA((4,))],
        limit=41 * 1024 * 1024,
    )
    margin_shape = ((3 * frames, HALF, width), BF16)
    places = {0: pltpu.SMEM, 4: pl.ANY}
    (edge,) = call(functools.partial(edge_kernel, True), [margin_shape], info, x, xa, xb, q, places=places)
    xo = swap(edge, "height", 1)
    q_side, k_side, v_side = call(
        side_kernel, [side_shape] * 3, xa, xb, wq, wk, wv, edge, places={5: pl.ANY}
    )
    (edge,) = call(functools.partial(edge_kernel, False), [margin_shape], info, x, xa, xb, k_side, places=places)
    xe = swap(edge, "height", 0)
    (ga_side,) = call(side_grad_kernel, [side_shape], ga, gb, wo, edge, places={3: pl.ANY})

    acc_shape = (groups, 5, 2 * HALF, GW)
    row_shape = ((2, groups, 2 * HALF, GW), BF16)
    stats, mixed, dq, dk, dv, k_row, v_row = call(
        forward_kernel,
        [((3 * groups, 4, GW), F32), own_shape, own_shape, (acc_shape, F32), (acc_shape, F32), row_shape, row_shape],
        info, xe, xo, wk, wv, q, ga_own, k, v, k_side, v_side, f_bias, ga_side,
        places={0: pltpu.SMEM, 12: pl.ANY},
        scratch=[pltpu.VMEM((2, groups, 6 * HALF, GW), BF16)] * 2,
    )
    sa = swap(stats, "tm", 1)
    sb = swap(stats, "tm", 0)
    token_shape = (frames, tokens, width)
    attended, dxq = call(middle_kernel, [(inputs.shape, BF16), ((3, 2 * HALF, width), F32)], mixed, dq, wo, wq)
    edge_shape = (frames, HALF, width)
    me, mo = call(
        margin_kernel,
        [(edge_shape, BF16)] * 2,
        info, sa, sb, q_side, ga_side, k_row, v_row, dk, dv, b_bias, wk, wv, dxq,
        places={0: pltpu.SMEM, 12: pl.ANY},
        scratch=[pltpu.VMEM((groups, 2, 2 * HALF, GW), BF16)] * 2 + [pltpu.VMEM((2, *edge_shape), BF16)],
    )
    ro = swap(mo, "height", 1)
    re = swap(me, "height", 0)
    (own,) = call(
        backward_kernel,
        [(token_shape, F32)],
        sa, sb, q_side, ga_side, k, v, dk, dv, dxq, b_bias, wk, wv,
        scratch=[pltpu.VMEM((groups, 3, 2 * HALF, GW), F32)] * 2,
    )
    (grad_in,) = call(
        last_kernel, [(inputs.shape, BF16)], info, own, re, ro,
        places={0: pltpu.SMEM}, scratch=[pltpu.VMEM(token_shape, F32)],
    )
    return (attended, grad_in)


def solution(mesh):
    placed = (P("tm", "height", None, None), P(), P(), P(), P(), P("tm", "height", None, None))
    return jax.shard_map(
        shards,
        mesh=mesh,
        in_specs=placed,
        out_specs=(P("tm", "height", None, None), P("tm", "height", None, None)),
        check_vma=False,
    )
```

```python
import functools

import jax
import jax.numpy as jnp
from jax import lax
from jax.experimental import pallas as pl
from jax.experimental.pallas import tpu as pltpu
from jax.sharding import PartitionSpec as P

HD = 64
RT = 2
RH = 7
BR = 8
WC = 4
GW = 256
HALF = BR * WC
PER = 4
VMEM_LIMIT = 28 * 1024 * 1024
NEG = -1e30
F32 = jnp.float32
BF16 = jnp.bfloat16


def nn(a, b):
    return lax.dot_general(a, b, (((1,), (0,)), ((), ())), preferred_element_type=F32)


def nt(a, b):
    return lax.dot_general(a, b, (((1,), (1,)), ((), ())), preferred_element_type=F32)


def tn(a, b):
    return lax.dot_general(a, b, (((0,), (0,)), ((), ())), preferred_element_type=F32)


def call(body, out_shapes, *args, places=None, scratch=(), limit=VMEM_LIMIT):
    places = places or {}
    return pl.pallas_call(
        body,
        out_shape=[jax.ShapeDtypeStruct(s, d) for s, d in out_shapes],
        in_specs=[pl.BlockSpec(memory_space=places.get(i, pltpu.VMEM)) for i in range(len(args))],
        out_specs=[pl.BlockSpec(memory_space=pltpu.VMEM) for _ in out_shapes],
        scratch_shapes=list(scratch),
        compiler_params=pltpu.CompilerParams(vmem_limit_bytes=limit),
    )(*args)


def store_blocks(y, out_ref, g):
    frames, blocks, half, _ = y.shape
    for b in range(blocks):
        for f in range(frames):
            at = slice((f % 2) * half, (f % 2 + 1) * half)
            if len(out_ref.shape) == 4:
                out_ref[g, b, at, :] = y[f, b]
            else:
                out_ref[g, f // 2, b, at, :] = y[f, b]


def project(x, w_ref, out_ref, scale=None):
    for g in range(out_ref.shape[0]):
        y = nn(x, w_ref[:, g * GW : (g + 1) * GW])
        if scale is not None:
            y = y * scale
        store_blocks(y.astype(BF16).reshape(-1, 3, HALF, GW), out_ref, g)


def project_t(x, w_ref, out_ref):
    for g in range(out_ref.shape[0]):
        y = nt(x, w_ref[g * GW : (g + 1) * GW, :])
        store_blocks(y.astype(BF16).reshape(-1, 3, HALF, GW), out_ref, g)


def flat(ref):
    return ref[...].reshape(-1, ref.shape[-1])


def own_kernel(
    n_frames, n_rows, frames, rows,
    info_ref, x_ref, gr_ref, wq_hbm, wk_hbm, wv_hbm, wo_hbm,
    q_ref, k_ref, v_ref, ga_ref, wq_ref, wk_ref, wv_ref, wo_ref, fb_ref, bb_ref,
    sem,
):
    pairs = ((wk_hbm, wk_ref), (wv_hbm, wv_ref), (wq_hbm, wq_ref), (wo_hbm, wo_ref))
    copies = [pltpu.make_async_copy(src, dst, sem.at[i]) for i, (src, dst) in enumerate(pairs)]
    for c in copies:
        c.start()
    tm, h = info_ref[0], info_ref[1]
    off_a, off_b = slot_offsets(tm)
    offsets = (off_a, off_a + 1, 0, 1, off_b, off_b + 1)
    for rb in range(3):
        for j in range(3):
            base = row_bias(rb, j, h, n_rows, rows)
            for s in range(6):
                at = (j * 6 + s) * HALF
                fb_ref[rb, at : at + HALF] = base + frame_bias(offsets[s], 0, tm, n_frames, frames)
            for p, off in enumerate((off_a, off_b)):
                for f in range(2):
                    at = (j * 2 + f) * HALF
                    bb_ref[p, rb, at : at + HALF] = base + frame_bias(f, off, tm, n_frames, frames)
    x = flat(x_ref)
    copies[0].wait()
    project(x, wk_ref, k_ref)
    copies[1].wait()
    project(x, wv_ref, v_ref)
    copies[2].wait()
    project(x, wq_ref, q_ref, HD**-0.5)
    copies[3].wait()
    project_t(flat(gr_ref), wo_ref, ga_ref)


def edge_kernel(for_odd, info_ref, x_ref, xa_ref, xb_ref, after_ref, out_ref):
    for parity in range(2):

        @pl.when(info_ref[1] % 2 == parity)
        def _(start=2 * HALF * (parity if for_odd else 1 - parity)):
            for s, ref in enumerate((xa_ref, x_ref, xb_ref)):
                out_ref[2 * s : 2 * s + 2] = ref[:, start : start + HALF]


def side_kernel(xa_ref, xb_ref, wq_ref, wk_ref, wv_ref, after_ref, q_ref, k_ref, v_ref):
    x = jnp.concatenate([flat(xa_ref), flat(xb_ref)], axis=0)
    project(x, wk_ref, k_ref)
    project(x, wv_ref, v_ref)
    project(x, wq_ref, q_ref, HD**-0.5)


def side_grad_kernel(ga_ref, gb_ref, wo_ref, after_ref, out_ref):
    project_t(jnp.concatenate([flat(ga_ref), flat(gb_ref)], axis=0), wo_ref, out_ref)


def spread(block):
    heads = block.shape[1] // HD
    lane = lax.broadcasted_iota(jnp.int32, block.shape, 1) // HD
    zero = jnp.zeros_like(block)
    return jnp.concatenate([jnp.where(lane == h, block, zero) for h in range(heads)], axis=0)


def row_bias(rb, j, h, n_rows, rows):
    w = j * BR + lax.broadcasted_iota(jnp.int32, (HALF, GW), 0) // WC
    r = (lax.broadcasted_iota(jnp.int32, (HALF, GW), 1) % HALF) // WC
    diff = w - r - BR
    glob = h * rows + rb * BR + w - BR
    ok = (diff >= -RH) & (diff <= RH) & (glob >= 0) & (glob < n_rows)
    return jnp.where(ok, F32(0), F32(NEG))


def frame_bias(key_off, query_off, tm, n_frames, frames):
    fq = (lax.broadcasted_iota(jnp.int32, (1, GW), 1) // HALF) % 2 + query_off
    diff = key_off - fq
    glob = tm * frames + key_off
    ok = (diff >= -RT) & (diff <= RT) & (glob >= 0) & (glob < n_frames)
    return jnp.where(ok, F32(0), F32(NEG))


def slot_offsets(tm):
    odd = tm % 2
    return 4 * odd - 2, 2 - 4 * odd


def pipeline(count, *stages):
    held = {}
    for t in range(count + len(stages) - 1):
        for s, stage in enumerate(stages):
            u = t - s
            if 0 <= u < count:
                held[u] = stage(u, held.get(u))


def forward_kernel(
    info_ref, xe_ref, xo_ref, wk_ref, wv_ref, q_ref, ga_ref, k_ref, v_ref, ks_ref, vs_ref, bias_ref, after_ref,
    stats_ref, mixed_ref, dq_ref, dk_ref, dv_ref, krow_ref, vrow_ref,
    kh_ref, vh_ref,
):
    groups = q_ref.shape[0]
    own = slice(2 * HALF, 4 * HALF)
    h_odd = info_ref[1] % 2
    for x_ref, side in ((xe_ref, 1 - h_odd), (xo_ref, h_odd)):
        x = flat(x_ref)
        for g in range(groups):
            kh_ref[side, g] = nn(x, wk_ref[:, g * GW : (g + 1) * GW]).astype(BF16)
            vh_ref[side, g] = nn(x, wv_ref[:, g * GW : (g + 1) * GW]).astype(BF16)
    for side in range(2):
        for g in range(groups):
            krow_ref[side, g] = kh_ref[side, g, own]
            vrow_ref[side, g] = vh_ref[side, g, own]
    diag = (
        lax.broadcasted_iota(jnp.int32, (GW, GW), 0) // HD == lax.broadcasted_iota(jnp.int32, (GW, GW), 1) // 64
    )

    def some(i, carry):
        cache = {}

        def blocks(g, which, margin_ref, side_ref, own_ref):
            if (g, which) not in cache:
                at = i * PER + g
                mid = [jnp.concatenate([side_ref[at, 0, b], own_ref[at, b], side_ref[at, 1, b]], axis=0) for b in range(3)]
                cache[g, which] = [margin_ref[0, at], *mid, margin_ref[1, at]]
            return cache[g, which]

        def flipped(g, which, b, block):
            if (g, which, b) not in cache:
                cache[g, which, b] = block.T
            return cache[g, which, b]

        def scores(u, _):
            g, rb = u // 3, u % 3
            kb = blocks(g, 0, kh_ref, ks_ref, k_ref)[rb : rb + 3]
            vb = blocks(g, 1, vh_ref, vs_ref, v_ref)[rb : rb + 3]
            kt = [flipped(g, 0, rb + j, kb[j]) for j in range(3)]
            vt = [flipped(g, 1, rb + j, vb[j]) for j in range(3)]
            qs, gs = spread(q_ref[i * PER + g, rb]), spread(ga_ref[i * PER + g, rb])
            s = nt(jnp.concatenate(kb, axis=0), qs)
            dp = nt(jnp.concatenate(vb, axis=0), gs)
            return kt, vt, qs, gs, s, dp

        def soft(u, held):
            rb = u % 3
            kt, vt, qs, gs, s, dp = held
            s = s + bias_ref[rb]
            m = jnp.max(s, axis=0, keepdims=True)
            e = jnp.exp(s - m)
            rl = 1.0 / jnp.sum(e, axis=0, keepdims=True)
            delta = jnp.sum(e * dp, axis=0, keepdims=True) * rl
            p = e * rl
            row = i * (3 * PER) + u
            stats_ref[row, 0:1, :] = m
            stats_ref[row, 1:2, :] = rl
            stats_ref[row, 2:3, :] = delta
            stats_ref[row, 3:4, :] = delta
            return kt, vt, qs, gs, p.astype(BF16), (p * (dp - delta)).astype(BF16)

        def back(u, held):
            g, rb = i * PER + u // 3, u % 3
            kt, vt, qs, gs, pb, ds = held

            def gather(t, p):
                parts = [nn(t[j], p[j * 6 * HALF : (j + 1) * 6 * HALF]) for j in range(3)]
                return parts[0] + parts[1] + parts[2]

            def fold(y):
                y = jnp.where(diag, y, 0.0)
                y = (y[:, : GW // 2] + y[:, GW // 2 :]).astype(BF16).T
                return y[:64] + y[64:]

            mixed_ref[g, rb] = fold(gather(vt, pb))
            dq_ref[g, rb] = fold(gather(kt, ds) * (HD**-0.5))

            def middle(p):
                return jnp.concatenate([p[(j * 6 + 2) * HALF : (j * 6 + 4) * HALF] for j in range(3)], axis=0)

            def add(ref, y):
                y = y.reshape(3, 2 * HALF, GW)
                if rb == 0:
                    ref[g, 0:3] = y
                else:
                    ref[g, rb : rb + 2] += y[:2]
                    ref[g, rb + 2] = y[2]

            add(dk_ref, nn(middle(ds), qs))
            add(dv_ref, nn(middle(pb), gs))

        pipeline(3 * PER, scores, soft, back)
        return carry

    lax.fori_loop(0, groups // PER, some, 0)


def unblock(y, out_ref):
    for b in range(3):
        for f in range(out_ref.shape[0]):
            part = y[b, f * HALF : (f + 1) * HALF].astype(out_ref.dtype)
            if len(out_ref.shape) == 3:
                out_ref[f, b * HALF : (b + 1) * HALF, :] = part
            else:
                out_ref[f, b * BR : (b + 1) * BR] = part.reshape(BR, WC, -1)


def middle_kernel(mixed_ref, dq_ref, wo_ref, wq_ref, att_ref, dxq_ref):
    groups = mixed_ref.shape[0]
    mixed = jnp.concatenate([flat(mixed_ref.at[g]) for g in range(groups)], axis=1)
    unblock(nn(mixed, wo_ref[...]).reshape(3, 2 * HALF, -1), att_ref)
    dq = jnp.concatenate([flat(dq_ref.at[g]) for g in range(groups)], axis=1)
    dxq_ref[...] = nt(dq, wq_ref[...]).reshape(dxq_ref.shape)


def margin_kernel(
    info_ref, sa_ref, sb_ref, qs_ref, gs_ref, krow_ref, vrow_ref, dk_ref, dv_ref, bias_ref, wk_ref, wv_ref, after_ref,
    me_ref, mo_ref,
    dka_ref, dva_ref, edge_ref,
):
    groups = qs_ref.shape[0]
    parts = {}

    def scores(u, _):
        g, side, p = u // 4, u // 2 % 2, u % 2
        qs, gs = spread(qs_ref[g, p, 2 * side]), spread(gs_ref[g, p, 2 * side])
        return qs, gs, nt(krow_ref[side, g], qs), nt(vrow_ref[side, g], gs)

    def soft(u, held):
        g, side, p = u // 4, u // 2 % 2, u % 2
        qs, gs, s, dp = held
        stat_ref, row = (sa_ref, sb_ref)[p], g * 3 + 2 * side
        m, rl, delta = stat_ref[row, 0:1, :], stat_ref[row, 1:2, :], stat_ref[row, 2:3, :]
        at = 4 * side * HALF
        pr = jnp.exp(s + bias_ref[p, 2 * side, at : at + 2 * HALF] - m) * rl
        return qs, gs, (pr * (dp - delta)).astype(BF16), pr.astype(BF16)

    def back(u, held):
        qs, gs, ds, pb = held
        parts[u] = nn(ds, qs), nn(pb, gs)

    pipeline(4 * groups, scores, soft, back)
    for g in range(groups):
        for side in range(2):
            u = 4 * g + 2 * side
            dka_ref[g, side] = (dk_ref[g, 4 * side] + parts[u][0] + parts[u + 1][0]).astype(BF16)
            dva_ref[g, side] = (dv_ref[g, 4 * side] + parts[u][1] + parts[u + 1][1]).astype(BF16)
    dk = jnp.concatenate([flat(dka_ref.at[g]) for g in range(groups)], axis=1)
    dv = jnp.concatenate([flat(dva_ref.at[g]) for g in range(groups)], axis=1)
    dx = (nt(dk, wk_ref[...]) + nt(dv, wv_ref[...])).astype(BF16)
    edge_ref[...] = dx.reshape(edge_ref.shape)
    h_odd = info_ref[1] % 2
    me_ref[...] = edge_ref[1 - h_odd]
    mo_ref[...] = edge_ref[h_odd]


def backward_kernel(
    sa_ref, sb_ref, qs_ref, gs_ref, k_ref, v_ref, dk_ref, dv_ref, dxq_ref, bias_ref, wk_ref, wv_ref,
    own_ref,
    dka_ref, dva_ref,
):
    groups = k_ref.shape[0]
    reach = ((0, 2, 2 * HALF), (0, 3, 0), (1, 3, 0))

    def group(g, carry):
        def scores(u, _):
            rb, p = u // 2, u % 2
            lo, hi, _ = reach[rb]
            qs, gs = spread(qs_ref[g, p, rb]), spread(gs_ref[g, p, rb])
            return qs, gs, nt(flat(k_ref.at[g, lo:hi]), qs), nt(flat(v_ref.at[g, lo:hi]), gs)

        def soft(u, held):
            rb, p = u // 2, u % 2
            qs, gs, s, dp = held
            stat_ref, row, at = (sa_ref, sb_ref)[p], g * 3 + rb, reach[rb][2]
            m, rl, delta = stat_ref[row, 0:1, :], stat_ref[row, 1:2, :], stat_ref[row, 2:3, :]
            pr = jnp.exp(s + bias_ref[p, rb, at : at + s.shape[0]] - m) * rl
            return qs, gs, pr.astype(BF16), (pr * (dp - delta)).astype(BF16)

        def back(u, held):
            lo, hi, _ = reach[u // 2]
            qs, gs, pb, ds = held

            def add(ref, first_ref, y):
                y = y.reshape(hi - lo, 2 * HALF, GW)
                if u == 0:
                    ref[g, 0:2] = first_ref[g, 1:3] + y
                elif u == 2:
                    ref[g, 0:2] += y[:2]
                    ref[g, 2] = first_ref[g, 3] + y[2]
                else:
                    ref[g, lo:hi] += y

            add(dka_ref, dk_ref, nn(ds, qs))
            add(dva_ref, dv_ref, nn(pb, gs))

        pipeline(6, scores, soft, back)
        return carry

    lax.fori_loop(0, groups, group, 0)
    dk = jnp.concatenate([flat(dka_ref.at[g]).astype(BF16) for g in range(groups)], axis=1)
    dv = jnp.concatenate([flat(dva_ref.at[g]).astype(BF16) for g in range(groups)], axis=1)
    dx = (nt(dk, wk_ref[...]) + nt(dv, wv_ref[...])).reshape(3, 2 * HALF, -1)
    unblock(dx + dxq_ref[...], own_ref)


def last_kernel(info_ref, own_ref, re_ref, ro_ref, out_ref, acc_ref):
    h_odd = info_ref[1] % 2
    top, bottom = slice(0, HALF), slice(2 * HALF, 3 * HALF)
    acc_ref[...] = own_ref[...]
    for parity, of_even, of_odd in ((0, bottom, top), (1, top, bottom)):

        @pl.when(h_odd == parity)
        def _(of_even=of_even, of_odd=of_odd):
            acc_ref[:, of_even] += re_ref[...].astype(F32)
            acc_ref[:, of_odd] += ro_ref[...].astype(F32)

    out_ref[...] = acc_ref[...].astype(BF16).reshape(out_ref.shape)


def swap_pairs(count, first):
    pairs = [(i, i + 1) for i in range(first, count - 1, 2)]
    return pairs + [(b, a) for a, b in pairs]


def swap(block, axis, first):
    return lax.ppermute(block, axis, swap_pairs(lax.axis_size(axis), first))


def shards(inputs, w_query, w_key, w_value, w_out, grad_out):
    frames, rows, cols, width = inputs.shape
    groups = width // GW
    tokens = rows * cols
    tm, h = lax.axis_index("tm"), lax.axis_index("height")
    n_frames, n_rows = lax.axis_size("tm") * frames, lax.axis_size("height") * rows
    info = jnp.stack([tm, h]).astype(jnp.int32)
    dims = (n_frames, n_rows, frames, rows)

    x = inputs.reshape(frames, tokens, width)
    xa = swap(x, "tm", 1)
    xb = swap(x, "tm", 0)
    grad = grad_out.reshape(frames, tokens, width)
    ga = swap(grad, "tm", 1)
    gb = swap(grad, "tm", 0)

    own_shape = ((groups, 3, 2 * HALF, GW), BF16)
    side_shape = ((groups, 2, 3, 2 * HALF, GW), BF16)
    weight_shape = (w_query.shape, BF16)
    hbm = {i: pltpu.HBM for i in range(3, 7)}
    q, k, v, ga_own, wq, wk, wv, wo, f_bias, b_bias = call(
        functools.partial(own_kernel, *dims),
        [own_shape] * 4 + [weight_shape] * 4 + [((3, 18 * HALF, GW), F32), ((2, 3, 6 * HALF, GW), F32)],
        info, x, grad, w_query, w_key, w_value, w_out,
        places={0: pltpu.SMEM, **hbm},
        scratch=[pltpu.SemaphoreType.DMA((4,))],
        limit=41 * 1024 * 1024,
    )
    margin_shape = ((3 * frames, HALF, width), BF16)
    places = {0: pltpu.SMEM, 4: pl.ANY}
    (edge,) = call(functools.partial(edge_kernel, True), [margin_shape], info, x, xa, xb, q, places=places)
    xo = swap(edge, "height", 1)
    q_side, k_side, v_side = call(
        side_kernel, [side_shape] * 3, xa, xb, wq, wk, wv, edge, places={5: pl.ANY}
    )
    (edge,) = call(functools.partial(edge_kernel, False), [margin_shape], info, x, xa, xb, k_side, places=places)
    xe = swap(edge, "height", 0)
    (ga_side,) = call(side_grad_kernel, [side_shape], ga, gb, wo, edge, places={3: pl.ANY})

    acc_shape = (groups, 5, 2 * HALF, GW)
    row_shape = ((2, groups, 2 * HALF, GW), BF16)
    stats, mixed, dq, dk, dv, k_row, v_row = call(
        forward_kernel,
        [((3 * groups, 4, GW), F32), own_shape, own_shape, (acc_shape, F32), (acc_shape, F32), row_shape, row_shape],
        info, xe, xo, wk, wv, q, ga_own, k, v, k_side, v_side, f_bias, ga_side,
        places={0: pltpu.SMEM, 12: pl.ANY},
        scratch=[pltpu.VMEM((2, groups, 6 * HALF, GW), BF16)] * 2,
    )
    sa = swap(stats, "tm", 1)
    sb = swap(stats, "tm", 0)
    token_shape = (frames, tokens, width)
    attended, dxq = call(middle_kernel, [(inputs.shape, BF16), ((3, 2 * HALF, width), F32)], mixed, dq, wo, wq)
    edge_shape = (frames, HALF, width)
    me, mo = call(
        margin_kernel,
        [(edge_shape, BF16)] * 2,
        info, sa, sb, q_side, ga_side, k_row, v_row, dk, dv, b_bias, wk, wv, dxq,
        places={0: pltpu.SMEM, 12: pl.ANY},
        scratch=[pltpu.VMEM((groups, 2, 2 * HALF, GW), BF16)] * 2 + [pltpu.VMEM((2, *edge_shape), BF16)],
    )
    ro = swap(mo, "height", 1)
    re = swap(me, "height", 0)
    (own,) = call(
        backward_kernel,
        [(token_shape, F32)],
        sa, sb, q_side, ga_side, k, v, dk, dv, dxq, b_bias, wk, wv,
        scratch=[pltpu.VMEM((groups, 3, 2 * HALF, GW), F32)] * 2,
    )
    (grad_in,) = call(
        last_kernel, [(inputs.shape, BF16)], info, own, re, ro,
        places={0: pltpu.SMEM}, scratch=[pltpu.VMEM(token_shape, F32)],
    )
    return (attended, grad_in)


def solution(mesh):
    placed = (P("tm", "height", None, None), P(), P(), P(), P(), P("tm", "height", None, None))
    return jax.shard_map(
        shards,
        mesh=mesh,
        in_specs=placed,
        out_specs=(P("tm", "height", None, None), P("tm", "height", None, None)),
        check_vma=False,
    )
```
